32 devices in a mesh: groups: 2 (over y), psg: 16 (over z, x, core).
Axes of the slice: x: 2, y: 2, z: 4, core: 2. Of those that a mesh axis runs over, the one named last changes fastest.
Arguments:
- tail_hidden_states: bfloat16 [256, 8192], P('groups', 'psg'), parts along dimension 0, may hold values from -6 to 6
- passage_hidden_states: bfloat16 [2048, 8192], P(('groups', 'psg')), parts along dimension 0, may hold values from -6 to 6
- lengths: int32 [4], P('groups'), parts along dimension 0, may hold values from 1 to 768, 1024 in all
- storage_order: int32 [4], P('groups'), parts along dimension 0, may hold values from 0 to 1, each once
- orders: int32 [6, 2], P('groups'), parts along dimension 0, may hold values from 0 to 1, each once within a row
- w_query: bfloat16 [8192, 4096], P('psg'), may hold values from -1 to 1
- key_weight: bfloat16 [8192, 512], P('psg'), may hold values from -0.0625 to 0.0625
- value_weight: bfloat16 [8192, 512], P('psg'), may hold values from -0.0625 to 0.0625
- w_out: bfloat16 [4096, 8192], P(None, 'psg'), may hold values from -0.09375 to 0.09375
- norm_gain: float32 [8192], P('psg'), may hold values from 0.1 to 1.9
Outputs:
- layer_out: bfloat16 [256, 8192], P('groups', 'psg'), parts along dimension 0
The draws below stay inside these ranges and needn't reach their ends.
There are 2 independent parts, one for each index of `groups`. The reference program is written for one: setup_inputs(seed, part) draws one part's arguments, and reference() takes and returns one part's arrays. A program takes and returns all parts, laid end to end along the dimension named above; an argument that names none is the same for every part. Nothing has to cross between parts.
Inputs may be any that keep to these rules, and one draw needn't show every extreme that they name: `lengths`: they sum to 1024; the largest is 768. `storage_order`: A permutation of the passages. `orders`: each row is a permutation of the passages.
All inputs are finite; a program needn't handle non-finite values.
Results may differ from the reference program's by a relative error of at most 0.01065.
The reference program's roundings to bfloat16 on the way count: a program that leaves them out, or rounds other values in their place, can miss the bound.
Values may be sent and summed in bfloat16 or wider, within the bound.
A program may use at most 128 MiB of HBM per device.

```python
import math
import jax
import jax.numpy as jnp
import numpy as np
from jax import lax

MODEL_WIDTH = 8192
QUERY_HEAD_COUNT = 32
KEY_VALUE_HEADS = 4
HEAD_SIZE = 128
TAIL_TOKENS = 128
PERMS = 3
LMAX = 768
PASSAGE_TOKENS = 1024
PASSAGES = 2


def draw_w_query(key, part):
    entry_key = jax.random.fold_in(key, 11)
    level_key = jax.random.fold_in(key, 12)
    order_key = jax.random.fold_in(key, 13)
    entries = jax.random.truncated_normal(entry_key, -6.0, 6.0, (MODEL_WIDTH, QUERY_HEAD_COUNT * HEAD_SIZE), jnp.float32)
    sharpest = 24.0
    ranks = jax.random.permutation(order_key, QUERY_HEAD_COUNT).astype(jnp.float32)
    jitter = jax.random.uniform(level_key, (QUERY_HEAD_COUNT,), jnp.float32)
    head_scale = jnp.exp((ranks + jitter) / QUERY_HEAD_COUNT * math.log(sharpest))
    column_scale = jnp.repeat(head_scale, HEAD_SIZE)
    scaled = entries * column_scale[None, :] / math.sqrt(MODEL_WIDTH)
    return jnp.clip(scaled, -1.0, 1.0).astype(jnp.bfloat16)


def shard_levels(stream_key, extent, shards, low, largest):
    def one(position, parts):
        steps = jax.random.uniform(jax.random.fold_in(jax.random.fold_in(stream_key, 6), position), (parts,), jnp.float32, low / len(shards), largest / len(shards))
        return jnp.repeat(jnp.exp(steps), extent[position] // parts).reshape((-1,) + (1,) * (len(extent) - position - 1))

    loudness = one(*shards[0])
    for cut in shards[1:]:
        loudness = loudness * one(*cut)
    return loudness


def split_up(number_of, total, most, skew):
    weights = [(1 << 20) // math.isqrt(grade ** skew) + 1 for grade in range(2, number_of + 1)]
    rest, given = total - most - (number_of - 1), [1] * (number_of - 1)
    while rest > 0:
        free = [i for i in range(number_of - 1) if given[i] < most]
        pool, budget = sum([weights[i] for i in free]), rest
        for i in free:
            addition = min(most - given[i], max(1, budget * weights[i] // pool), rest)
            given[i] = given[i] + addition
            rest = rest - addition
    return np.array([most] + given)


def ragged_sizes(own_key, amount, total, limit, skew):
    if amount == 2:
        one = jax.random.randint(own_key, (), max(1, total - limit), min(limit, total - 1) + 1)
        return jnp.stack([one, total - one])
    sizes = jnp.asarray(split_up(amount, total, limit, skew), jnp.int32)
    couples = (amount - 1) // 2
    donor, taker = sizes[1:1 + 2 * couples:2], sizes[2:2 + 2 * couples:2]
    slack = jnp.minimum(donor - 1, limit - taker)
    passed = jax.random.randint(jax.random.fold_in(own_key, 1), (couples,), 0, 1 << 20) % (slack + 1)
    sizes = sizes.at[1:1 + 2 * couples:2].set(donor - passed).at[2:2 + 2 * couples:2].set(taker + passed)
    return sizes[jax.random.permutation(jax.random.fold_in(own_key, 2), amount)]


def gaussian(key, extent, scale, reach, split=(), kind=jnp.bfloat16):
    result = jax.random.normal(key, extent, jnp.float32) * scale
    if len(split) > 0:
        result = shard_levels(key, extent, split, -0.22, 0.18) * result
    return jnp.clip(result, min=-reach, max=reach).astype(kind)


def setup_inputs(seed: int = 0, part: int = 0) -> dict:
    streams_of = jax.random.split(jax.random.key(seed), 11)
    part_keys = jax.random.split(jax.random.fold_in(streams_of[10], part), 11)
    return {
        "tail_hidden_states": gaussian(part_keys[0], (TAIL_TOKENS, MODEL_WIDTH), 1.0, 6.0, ((1, 16),)),
        "passage_hidden_states": gaussian(part_keys[1], (PASSAGE_TOKENS, MODEL_WIDTH), 1.0, 6.0, ((0, 16),)),
        "lengths": ragged_sizes(part_keys[2], PASSAGES, PASSAGE_TOKENS, LMAX, 2).astype(jnp.int32),
        "storage_order": jax.random.permutation(part_keys[3], PASSAGES).astype(jnp.int32),
        "orders": jax.vmap(lambda own: jax.random.permutation(own, PASSAGES))(jax.random.split(part_keys[4], PERMS)).reshape((PERMS, PASSAGES)).astype(jnp.int32),
        "w_query": draw_w_query(jax.random.fold_in(streams_of[10], 71), part),
        "key_weight": gaussian(streams_of[6], (MODEL_WIDTH, KEY_VALUE_HEADS * HEAD_SIZE), MODEL_WIDTH ** -0.5, 0.0625, ((0, 16),)),
        "value_weight": gaussian(streams_of[7], (MODEL_WIDTH, KEY_VALUE_HEADS * HEAD_SIZE), MODEL_WIDTH ** -0.5, 0.0625, ((0, 16),)),
        "w_out": gaussian(streams_of[8], (QUERY_HEAD_COUNT * HEAD_SIZE, MODEL_WIDTH), (QUERY_HEAD_COUNT * HEAD_SIZE) ** -0.5, 0.09375, ((1, 16),)),
        "norm_gain": jnp.clip(1.0 + 0.18 * jax.random.normal(streams_of[9], (MODEL_WIDTH,), jnp.float32), 0.1, 1.9),
    }


theta_base = 500000.0
epsilon = 1e-05

def rotate(vectors, places):
    half = vectors.shape[-1] // 2
    freqs = theta_base ** (-jnp.arange(half, dtype=jnp.float32) * 2.0 / vectors.shape[-1])
    angles = places.astype(jnp.float32)[:, None] * freqs[None, :]
    cosine = jnp.cos(angles)[:, None, :]
    sine = jnp.sin(angles)[:, None, :]
    first = vectors[..., :half]
    second = vectors[..., half:]
    return jnp.concatenate([first * cosine - second * sine, second * cosine + first * sine], axis=-1)

def key_positions(lengths, storage_order, orders):
    passages = lengths.shape[0]
    stored_lengths = lengths[storage_order]
    ends = jnp.cumsum(stored_lengths).astype(jnp.int32)
    starts = (ends - stored_lengths).astype(jnp.int32)
    row_ids = jnp.arange(PASSAGE_TOKENS, dtype=jnp.int32)
    slots = lax.optimization_barrier(jnp.sum((ends[None, :] <= row_ids[:, None]).astype(jnp.int32), axis=1))
    passage_of = storage_order[slots]
    offsets = row_ids - starts[slots]
    ordered = lengths[orders]
    order_starts = (jnp.cumsum(ordered, axis=1) - ordered).astype(jnp.int32)
    order_ids = jnp.arange(orders.shape[0], dtype=jnp.int32)[:, None]
    placed = jnp.zeros((orders.shape[0], passages), jnp.int32).at[order_ids, orders].set(order_starts)
    return placed[:, passage_of] + offsets[None, :]

def reference(tail_hidden_states, passage_hidden_states, lengths, storage_order, orders, w_query, key_weight, value_weight, w_out, norm_gain):
    query_group = QUERY_HEAD_COUNT // KEY_VALUE_HEADS
    tail_pos = PASSAGE_TOKENS + jnp.arange(TAIL_TOKENS, dtype=jnp.int32)
    query_vectors = jnp.dot(tail_hidden_states, w_query, preferred_element_type=jnp.float32).reshape(TAIL_TOKENS, QUERY_HEAD_COUNT, HEAD_SIZE)
    query_vectors = rotate(query_vectors, tail_pos).astype(jnp.bfloat16)
    query_vectors = lax.optimization_barrier(query_vectors).astype(jnp.float32).reshape(TAIL_TOKENS, KEY_VALUE_HEADS, query_group, HEAD_SIZE)
    tail_key_rows = jnp.dot(tail_hidden_states, key_weight, preferred_element_type=jnp.float32).reshape(TAIL_TOKENS, KEY_VALUE_HEADS, HEAD_SIZE)
    tail_key_rows = lax.optimization_barrier(rotate(tail_key_rows, tail_pos).astype(jnp.bfloat16)).astype(jnp.float32)
    tail_value_rows = jnp.dot(tail_hidden_states, value_weight, preferred_element_type=jnp.float32).astype(jnp.bfloat16)
    tail_value_rows = lax.optimization_barrier(tail_value_rows).astype(jnp.float32).reshape(TAIL_TOKENS, KEY_VALUE_HEADS, HEAD_SIZE)
    unrotated_key = jnp.dot(passage_hidden_states, key_weight, preferred_element_type=jnp.float32).reshape(PASSAGE_TOKENS, KEY_VALUE_HEADS, HEAD_SIZE)
    passage_values = jnp.dot(passage_hidden_states, value_weight, preferred_element_type=jnp.float32).astype(jnp.bfloat16)
    passage_values = lax.optimization_barrier(passage_values).astype(jnp.float32).reshape(PASSAGE_TOKENS, KEY_VALUE_HEADS, HEAD_SIZE)
    token_positions = key_positions(lengths, storage_order, orders)
    scale = HEAD_SIZE ** (-0.5)
    tail_scores = jnp.einsum('tkgd,skd->tkgs', query_vectors, tail_key_rows) * scale
    causal = jnp.arange(TAIL_TOKENS)[None, :] <= jnp.arange(TAIL_TOKENS)[:, None]
    tail_scores = jnp.where(causal[:, None, None, :], tail_scores, -1e+30)

    def single_ordering(running, places):
        keys = lax.optimization_barrier(rotate(unrotated_key, places).astype(jnp.bfloat16)).astype(jnp.float32)
        scores = jnp.einsum('tkgd,nkd->tkgn', query_vectors, keys) * scale
        peak = jnp.maximum(lax.optimization_barrier(jnp.max(scores, axis=-1)), lax.optimization_barrier(jnp.max(tail_scores, axis=-1)))[..., None]
        weights = jnp.exp(scores - peak)
        tail_weights = jnp.exp(tail_scores - peak)
        denom = lax.optimization_barrier(jnp.sum(weights, axis=-1)) + lax.optimization_barrier(jnp.sum(tail_weights, axis=-1))
        weights_b = lax.optimization_barrier(weights.astype(jnp.bfloat16)).astype(jnp.float32)
        tail_b = lax.optimization_barrier(tail_weights.astype(jnp.bfloat16)).astype(jnp.float32)
        numer = jnp.einsum('tkgn,nkd->tkgd', weights_b, passage_values) + jnp.einsum('tkgs,skd->tkgd', tail_b, tail_value_rows)
        return (running + numer / denom[..., None], None)
    agreed_output, unused_slot = lax.scan(single_ordering, jnp.zeros((TAIL_TOKENS, KEY_VALUE_HEADS, query_group, HEAD_SIZE), jnp.float32), token_positions)
    mixed = agreed_output.reshape(TAIL_TOKENS, QUERY_HEAD_COUNT * HEAD_SIZE).astype(jnp.bfloat16)
    projected = jnp.dot(mixed, w_out, preferred_element_type=jnp.float32)
    factor = lax.rsqrt(lax.optimization_barrier(jnp.mean(projected * projected, axis=1, keepdims=True)) + epsilon)
    return (projected * factor * norm_gain[None, :]).astype(jnp.bfloat16)
```

```python
import jax
import jax.numpy as jnp
from jax import lax
from jax.sharding import PartitionSpec as P

MODEL_WIDTH = 8192
HEAD_SIZE = 128


theta_base = 500000.0
epsilon = 1e-05


def joined(part, axis, combine):
    gathered = jax.tree.map(lambda a: lax.all_gather(a, axis), part)

    def take(source):
        return jax.tree.map(lambda a: lax.dynamic_index_in_dim(a, source, 0, False), gathered)

    return lax.fori_loop(
        1, lax.axis_size(axis), lambda source, state: combine(state, take(source)), take(0)
    )


def rotate(vectors, places):
    half = vectors.shape[-1] // 2
    freqs = theta_base ** (-jnp.arange(half, dtype=jnp.float32) * 2.0 / vectors.shape[-1])
    angles = places.astype(jnp.float32)[:, None] * freqs[None, :]
    cosine = jnp.cos(angles)[:, None, :]
    sine = jnp.sin(angles)[:, None, :]
    first = vectors[..., :half]
    second = vectors[..., half:]
    return jnp.concatenate(
        [first * cosine - second * sine, second * cosine + first * sine], axis=-1
    )


def running_sum(values):
    count = values.shape[-1]
    earlier = (jnp.arange(count)[None, :] <= jnp.arange(count)[:, None]).astype(values.dtype)
    return jnp.sum(earlier * values[..., None, :], axis=-1)


def token_places(lengths, storage_order, orders, row_ids):
    numbers = jnp.arange(lengths.shape[0], dtype=jnp.int32)
    pick = (storage_order[:, None] == numbers[None, :]).astype(jnp.int32)
    stored_lengths = jnp.sum(pick * lengths[None, :], axis=1)
    ends = running_sum(stored_lengths)
    starts = ends - stored_lengths
    slots = jnp.sum((ends[None, :] <= row_ids[:, None]).astype(jnp.int32), axis=1)
    in_slot = (slots[:, None] == numbers[None, :]).astype(jnp.int32)
    offsets = row_ids - jnp.sum(in_slot * starts[None, :], axis=1)
    passage_hot = jnp.sum(in_slot[:, :, None] * pick[None, :, :], axis=1)
    ordered_hot = (orders[:, :, None] == numbers[None, None, :]).astype(jnp.int32)
    ordered_lengths = jnp.sum(ordered_hot * lengths[None, None, :], axis=2)
    order_starts = running_sum(ordered_lengths) - ordered_lengths
    placed = jnp.sum(ordered_hot * order_starts[:, :, None], axis=1)
    return jnp.sum(passage_hot[None, :, :] * placed[:, None, :], axis=2) + offsets[None, :]


def by_heads(
    tail_hidden_states,
    passage_hidden_states,
    lengths,
    storage_order,
    orders,
    w_query,
    key_weight,
    value_weight,
    w_out,
    norm_gain,
):
    shards = lax.axis_size("psg")
    device = lax.axis_index("psg")
    row_count, width = passage_hidden_states.shape
    tail_count, depth = tail_hidden_states.shape
    kv_heads = key_weight.shape[1] // HEAD_SIZE
    own_heads = w_query.shape[1] // HEAD_SIZE // shards
    share = shards // kv_heads
    total_keys = row_count * shards
    rows = total_keys // share
    tail_rows = tail_count // share
    perms = orders.shape[0]
    place = device % share

    query_part = jnp.einsum(
        "td,dsc->stc",
        tail_hidden_states,
        w_query.reshape(depth, shards, own_heads * HEAD_SIZE),
        preferred_element_type=jnp.float32,
    )
    query_sum = lax.psum_scatter(query_part, "psg", scatter_dimension=0)
    slab = lax.all_to_all(passage_hidden_states, "psg", 1, 0, tiled=True)
    slab = jnp.concatenate(
        [slab.reshape(share, rows, depth), tail_hidden_states.reshape(share, tail_rows, depth)],
        axis=1,
    )
    both = jnp.concatenate(
        [
            key_weight.reshape(depth, kv_heads, HEAD_SIZE),
            value_weight.reshape(depth, kv_heads, HEAD_SIZE),
        ],
        axis=2,
    )
    pair_part = jnp.einsum("rnd,dkc->krnc", slab, both, preferred_element_type=jnp.float32)
    pair_sum = lax.psum_scatter(
        pair_part.reshape(shards, rows + tail_rows, 2 * HEAD_SIZE), "psg", scatter_dimension=0
    )

    tail_pos = total_keys + jnp.arange(tail_count, dtype=jnp.int32)
    query = rotate(query_sum.reshape(tail_count, own_heads, HEAD_SIZE), tail_pos)
    query = query.astype(jnp.bfloat16)
    own_rows = place * rows + jnp.arange(rows, dtype=jnp.int32)
    places = token_places(lengths, storage_order, orders, own_rows)
    own_tail = total_keys + place * tail_rows + jnp.arange(tail_rows, dtype=jnp.int32)
    raw_key = pair_sum[:, :HEAD_SIZE]
    unrotated = jnp.concatenate([raw_key[:rows]] * perms + [raw_key[rows:]])
    spots = jnp.concatenate([places.reshape(-1), own_tail])
    own_keys = rotate(unrotated[:, None, :], spots)[:, 0, :].astype(jnp.bfloat16)
    own_values = pair_sum[:, HEAD_SIZE:].astype(jnp.bfloat16)
    packed = jnp.concatenate([own_keys, own_values])
    alike = [[k * share + i for i in range(share)] for k in range(kv_heads)]
    every = lax.all_gather(packed, "psg", axis_index_groups=alike)
    cut = perms * rows
    keys = every[:, :cut].reshape(share, perms, rows, HEAD_SIZE)
    tail_keys = every[:, cut : cut + tail_rows].reshape(tail_count, HEAD_SIZE)
    low = cut + tail_rows
    values = every[:, low : low + rows].reshape(total_keys, HEAD_SIZE)
    tail_values = every[:, low + rows :].reshape(tail_count, HEAD_SIZE)

    scale = HEAD_SIZE ** (-0.5)
    scores = (
        jnp.einsum("tgd,spnd->ptgsn", query, keys, preferred_element_type=jnp.float32) * scale
    ).reshape(perms, tail_count, own_heads, total_keys)
    tail_scores = (
        jnp.einsum("tgd,sd->tgs", query, tail_keys, preferred_element_type=jnp.float32) * scale
    )
    causal = jnp.arange(tail_count)[None, :] <= jnp.arange(tail_count)[:, None]
    tail_scores = jnp.where(causal[:, None, :], tail_scores, -1e30)
    peak = jnp.maximum(jnp.max(scores, axis=-1), jnp.max(tail_scores, axis=-1))[..., None]
    weights = jnp.exp(scores - peak)
    tail_weights = jnp.exp(tail_scores - peak)
    denom = jnp.sum(weights, axis=-1) + jnp.sum(tail_weights, axis=-1)
    numer = jnp.einsum(
        "ptgn,nd->ptgd", weights.astype(jnp.bfloat16), values, preferred_element_type=jnp.float32
    ) + jnp.einsum(
        "ptgs,sd->ptgd",
        tail_weights.astype(jnp.bfloat16),
        tail_values,
        preferred_element_type=jnp.float32,
    )
    agreed = jnp.sum(numer / denom[..., None], axis=0)
    own_mixed = agreed.reshape(tail_count, own_heads * HEAD_SIZE).astype(jnp.bfloat16)
    mixed = lax.all_gather(own_mixed, "psg", axis=1, tiled=True)
    projected = jnp.dot(mixed, w_out, preferred_element_type=jnp.float32)
    squares = lax.psum(jnp.sum(projected * projected, axis=1), "psg")
    factor = lax.rsqrt(squares / width + epsilon)[:, None]
    return (projected * factor * norm_gain[None, :]).astype(jnp.bfloat16)


def by_rows(
    tail_hidden_states,
    passage_hidden_states,
    lengths,
    storage_order,
    orders,
    w_query,
    key_weight,
    value_weight,
    w_out,
    norm_gain,
):
    shards = lax.axis_size("psg")
    device = lax.axis_index("psg")
    row_count = passage_hidden_states.shape[0]
    tail_count = tail_hidden_states.shape[0]
    kv_heads = key_weight.shape[1] // HEAD_SIZE
    query_heads = w_query.shape[1] // HEAD_SIZE
    query_group = query_heads // kv_heads
    total_keys = row_count * shards
    query_part = jnp.dot(tail_hidden_states, w_query, preferred_element_type=jnp.float32)
    key_part = jnp.dot(tail_hidden_states, key_weight, preferred_element_type=jnp.float32)
    value_part = jnp.dot(tail_hidden_states, value_weight, preferred_element_type=jnp.float32)
    query_sum, key_sum, value_sum = lax.psum((query_part, key_part, value_part), "psg")
    tail_pos = total_keys + jnp.arange(tail_count, dtype=jnp.int32)
    query_vectors = rotate(query_sum.reshape(tail_count, query_heads, HEAD_SIZE), tail_pos).astype(
        jnp.bfloat16
    )
    query_vectors = query_vectors.reshape(tail_count, kv_heads, query_group, HEAD_SIZE)
    tail_key_rows = rotate(key_sum.reshape(tail_count, kv_heads, HEAD_SIZE), tail_pos).astype(
        jnp.bfloat16
    )
    tail_value_rows = value_sum.astype(jnp.bfloat16).reshape(tail_count, kv_heads, HEAD_SIZE)

    def add_block(piece):
        return jnp.dot(passage_hidden_states, piece, preferred_element_type=jnp.float32)

    unrotated_key = add_block(lax.all_gather(key_weight, "psg", axis=0, tiled=True))
    raw_value = add_block(lax.all_gather(value_weight, "psg", axis=0, tiled=True))
    row_ids = device * row_count + jnp.arange(row_count, dtype=jnp.int32)
    token_positions = token_places(lengths, storage_order, orders, row_ids)
    passage_values = raw_value.astype(jnp.bfloat16).reshape(row_count, kv_heads, HEAD_SIZE)
    unrotated_key = unrotated_key.reshape(row_count, kv_heads, HEAD_SIZE)
    scale = HEAD_SIZE ** (-0.5)
    tail_scores = (
        jnp.einsum(
            "tkgd,skd->tkgs", query_vectors, tail_key_rows, preferred_element_type=jnp.float32
        )
        * scale
    )
    causal = jnp.arange(tail_count)[None, :] <= jnp.arange(tail_count)[:, None]
    tail_scores = jnp.where(causal[:, None, None, :], tail_scores, -1e30)
    tail_top = jnp.max(tail_scores, axis=-1)

    def scores_for(places):
        keys = rotate(unrotated_key, places).astype(jnp.bfloat16)
        return (
            jnp.einsum("tkgd,nkd->tkgn", query_vectors, keys, preferred_element_type=jnp.float32)
            * scale
        )

    def local_stats(places):
        scores = scores_for(places)
        peak = jnp.maximum(jnp.max(scores, axis=-1), tail_top)
        return (peak, jnp.sum(jnp.exp(scores - peak[..., None]), axis=-1))

    def combine(first, second):
        peak = jnp.maximum(first[0], second[0])
        return (peak, first[1] * jnp.exp(first[0] - peak) + second[1] * jnp.exp(second[0] - peak))

    peaks, totals = joined(lax.map(local_stats, token_positions), "psg", combine)

    def accumulate(running, inputs):
        places, peak, partial_value = inputs
        weights = jnp.exp(scores_for(places) - peak[..., None])
        tail_weights = jnp.exp(tail_scores - peak[..., None])
        denom = (partial_value + jnp.sum(tail_weights, axis=-1))[..., None]
        shared = jnp.einsum(
            "tkgn,nkd->tkgd",
            weights.astype(jnp.bfloat16),
            passage_values,
            preferred_element_type=jnp.float32,
        )
        own = jnp.einsum(
            "tkgs,skd->tkgd",
            tail_weights.astype(jnp.bfloat16),
            tail_value_rows,
            preferred_element_type=jnp.float32,
        )
        return ((running[0] + shared / denom, running[1] + own / denom), None)

    start_sums = jnp.zeros((tail_count, kv_heads, query_group, HEAD_SIZE), jnp.float32)
    (shared_sum, own_sum), unused_slot = lax.scan(
        accumulate, (start_sums, start_sums), (token_positions, peaks, totals)
    )
    agreed_output = lax.psum(shared_sum, "psg") + own_sum
    mixed = agreed_output.reshape(tail_count, -1).astype(jnp.bfloat16)
    projected = jnp.dot(mixed, w_out, preferred_element_type=jnp.float32)
    squares = lax.psum(jnp.sum(projected * projected, axis=1), "psg")
    factor = lax.rsqrt(squares / MODEL_WIDTH + epsilon)[:, None]
    return (projected * factor * norm_gain[None, :]).astype(jnp.bfloat16)


def per_device(*arrays):
    tail_hidden_states, w_query, key_weight = arrays[0], arrays[5], arrays[6]
    shards = lax.axis_size("psg")
    query_heads = w_query.shape[1] // HEAD_SIZE
    kv_heads = key_weight.shape[1] // HEAD_SIZE
    fits = query_heads % shards == 0 and shards % kv_heads == 0
    if fits and tail_hidden_states.shape[0] % (shards // kv_heads) == 0:
        return by_heads(*arrays)
    return by_rows(*arrays)


def solution(mesh):
    placed = (
        P("groups", "psg"),
        P(("groups", "psg"), None),
        P("groups"),
        P("groups"),
        P("groups", None),
        P("psg", None),
        P("psg", None),
        P("psg", None),
        P(None, "psg"),
        P("psg"),
    )
    return jax.shard_map(
        per_device, mesh=mesh, in_specs=placed, out_specs=P("groups", "psg"), check_vma=False
    )
```

```python
import functools

import jax
import jax.numpy as jnp
from jax import lax
from jax.experimental import pallas as pl
from jax.experimental.pallas import tpu as pltpu
from jax.sharding import PartitionSpec as P

MODEL_WIDTH = 8192
HEAD_SIZE = 128


theta_base = 500000.0
epsilon = 1e-05


def joined(part, axis, combine):
    gathered = jax.tree.map(lambda a: lax.all_gather(a, axis), part)

    def take(source):
        return jax.tree.map(lambda a: lax.dynamic_index_in_dim(a, source, 0, False), gathered)

    return lax.fori_loop(
        1, lax.axis_size(axis), lambda source, state: combine(state, take(source)), take(0)
    )


def rotate(vectors, places):
    half = vectors.shape[-1] // 2
    freqs = theta_base ** (-jnp.arange(half, dtype=jnp.float32) * 2.0 / vectors.shape[-1])
    angles = places.astype(jnp.float32)[:, None] * freqs[None, :]
    cosine = jnp.cos(angles)[:, None, :]
    sine = jnp.sin(angles)[:, None, :]
    first = vectors[..., :half]
    second = vectors[..., half:]
    return jnp.concatenate(
        [first * cosine - second * sine, second * cosine + first * sine], axis=-1
    )


def running_sum(values):
    count = values.shape[-1]
    earlier = (jnp.arange(count)[None, :] <= jnp.arange(count)[:, None]).astype(values.dtype)
    return jnp.sum(earlier * values[..., None, :], axis=-1)


def token_places(lengths, storage_order, orders, row_ids):
    numbers = jnp.arange(lengths.shape[0], dtype=jnp.int32)
    pick = (storage_order[:, None] == numbers[None, :]).astype(jnp.int32)
    stored_lengths = jnp.sum(pick * lengths[None, :], axis=1)
    ends = running_sum(stored_lengths)
    starts = ends - stored_lengths
    slots = jnp.sum((ends[None, :] <= row_ids[:, None]).astype(jnp.int32), axis=1)
    in_slot = (slots[:, None] == numbers[None, :]).astype(jnp.int32)
    offsets = row_ids - jnp.sum(in_slot * starts[None, :], axis=1)
    passage_hot = jnp.sum(in_slot[:, :, None] * pick[None, :, :], axis=1)
    ordered_hot = (orders[:, :, None] == numbers[None, None, :]).astype(jnp.int32)
    ordered_lengths = jnp.sum(ordered_hot * lengths[None, None, :], axis=2)
    order_starts = running_sum(ordered_lengths) - ordered_lengths
    placed = jnp.sum(ordered_hot * order_starts[:, :, None], axis=1)
    return jnp.sum(passage_hot[None, :, :] * placed[:, None, :], axis=2) + offsets[None, :]


def backwards(index, bits):
    return sum((index // 2**b) % 2 * 2 ** (bits - 1 - b) for b in range(bits))


def closing_kernel(
    bits, width, own_ref, w_ref, gain_ref, out_ref, held, total, given, got, sends, lands
):
    me = lax.axis_index("psg")
    partners = [me + (1 - 2 * ((me // 2**b) % 2)) * 2**b for b in reversed(range(bits))]
    barrier = pltpu.get_barrier_semaphore()
    for partner in partners:
        pl.semaphore_signal(
            barrier, inc=1, device_id={"psg": partner}, device_id_type=pl.DeviceIdType.MESH
        )
    pl.semaphore_wait(barrier, bits)

    slot = backwards(me, bits)
    held[slot] = own_ref[...]
    for step, partner in enumerate(partners):
        run = pl.ds(slot // 2**step * 2**step, 2**step)
        copy = pltpu.make_async_remote_copy(
            src_ref=held.at[run],
            dst_ref=held.at[run],
            send_sem=sends.at[step],
            recv_sem=lands.at[step],
            device_id={"psg": partner},
            device_id_type=pl.DeviceIdType.MESH,
        )
        copy.start()
        copy.wait()
    part = own_ref.shape[1]
    for j in range(2**bits):
        product = jnp.dot(
            held[backwards(j, bits)],
            w_ref[j * part : (j + 1) * part, :],
            preferred_element_type=jnp.float32,
        )
        if j == 0:
            total[...] = product
        else:
            total[...] += product

    projected = total[...]
    squared = projected * projected
    folded = sum(squared[:, c : c + 128] for c in range(0, squared.shape[1], 128))
    sums = jnp.sum(folded.T, axis=0, keepdims=True)
    for step, partner in enumerate(partners):
        given[step] = jnp.broadcast_to(sums, given.shape[1:])
        copy = pltpu.make_async_remote_copy(
            src_ref=given.at[step],
            dst_ref=got.at[step],
            send_sem=sends.at[bits + step],
            recv_sem=lands.at[bits + step],
            device_id={"psg": partner},
            device_id_type=pl.DeviceIdType.MESH,
        )
        copy.start()
        copy.wait()
        sums = sums + got[step][:1]
    spread = jnp.broadcast_to(sums, (128, sums.shape[1])).T
    factor = lax.rsqrt(spread / width + epsilon)
    for c in range(0, projected.shape[1], 128):
        out_ref[:, c : c + 128] = (
            projected[:, c : c + 128] * factor * gain_ref[:, c : c + 128]
        ).astype(jnp.bfloat16)


def closing(own_mixed, w_out, norm_gain, shards, width):
    bits = shards.bit_length() - 1
    tail_count, columns = own_mixed.shape[0], w_out.shape[1]
    return pl.pallas_call(
        functools.partial(closing_kernel, bits, width),
        out_shape=jax.ShapeDtypeStruct((tail_count, columns), jnp.bfloat16),
        in_specs=[pl.BlockSpec(memory_space=pltpu.VMEM)] * 3,
        out_specs=pl.BlockSpec(memory_space=pltpu.VMEM),
        scratch_shapes=[
            pltpu.VMEM((shards, *own_mixed.shape), jnp.bfloat16),
            pltpu.VMEM((tail_count, columns), jnp.float32),
            pltpu.VMEM((bits, 8, tail_count), jnp.float32),
            pltpu.VMEM((bits, 8, tail_count), jnp.float32),
            pltpu.SemaphoreType.DMA((2 * bits,)),
            pltpu.SemaphoreType.DMA((2 * bits,)),
        ],
        compiler_params=pltpu.CompilerParams(
            collective_id=0, has_side_effects=True, vmem_limit_bytes=32 * 2**20
        ),
    )(own_mixed, w_out, norm_gain[None, :])


def pair_kernel(slab_ref, key_ref, value_ref, out_ref):
    both = jnp.concatenate([key_ref[...], value_ref[...]], axis=1)
    out_ref[0] = jnp.dot(slab_ref[...], both, preferred_element_type=jnp.float32)


def pair_products(slab, key_weight, value_weight):
    count, depth = slab.shape
    kv_heads = key_weight.shape[1] // HEAD_SIZE
    column = pl.BlockSpec((depth, HEAD_SIZE), lambda k: (0, k))
    return pl.pallas_call(
        pair_kernel,
        grid=(kv_heads,),
        out_shape=jax.ShapeDtypeStruct((kv_heads, count, 2 * HEAD_SIZE), jnp.float32),
        in_specs=[pl.BlockSpec((count, depth), lambda k: (0, 0)), column, column],
        out_specs=pl.BlockSpec((1, count, 2 * HEAD_SIZE), lambda k: (k, 0, 0)),
        compiler_params=pltpu.CompilerParams(vmem_limit_bytes=32 * 2**20),
    )(slab, key_weight, value_weight)


def by_heads(
    tail_hidden_states,
    passage_hidden_states,
    lengths,
    storage_order,
    orders,
    w_query,
    key_weight,
    value_weight,
    w_out,
    norm_gain,
):
    shards = lax.axis_size("psg")
    device = lax.axis_index("psg")
    row_count, width = passage_hidden_states.shape
    tail_count, depth = tail_hidden_states.shape
    kv_heads = key_weight.shape[1] // HEAD_SIZE
    own_heads = w_query.shape[1] // HEAD_SIZE // shards
    share = shards // kv_heads
    total_keys = row_count * shards
    rows = total_keys // share
    tail_rows = tail_count // share
    perms = orders.shape[0]
    place = device % share

    query_part = jnp.einsum(
        "td,dsc->stc",
        tail_hidden_states,
        w_query.reshape(depth, shards, own_heads * HEAD_SIZE),
        preferred_element_type=jnp.float32,
    )
    query_part, passage_hidden_states = lax.optimization_barrier(
        (query_part, passage_hidden_states)
    )
    query_sum = lax.psum_scatter(query_part, "psg", scatter_dimension=0)
    slab = lax.all_to_all(passage_hidden_states, "psg", 1, 0, tiled=True)
    slab = jnp.concatenate(
        [slab.reshape(share, rows, depth), tail_hidden_states.reshape(share, tail_rows, depth)],
        axis=1,
    )
    pair_part = pair_products(slab.reshape(-1, depth), key_weight, value_weight)
    pair_sum = lax.psum_scatter(
        pair_part.reshape(shards, rows + tail_rows, 2 * HEAD_SIZE), "psg", scatter_dimension=0
    )

    tail_pos = total_keys + jnp.arange(tail_count, dtype=jnp.int32)
    query = rotate(query_sum.reshape(tail_count, own_heads, HEAD_SIZE), tail_pos)
    query = query.astype(jnp.bfloat16)
    own_rows = place * rows + jnp.arange(rows, dtype=jnp.int32)
    places = token_places(lengths, storage_order, orders, own_rows)
    own_tail = total_keys + place * tail_rows + jnp.arange(tail_rows, dtype=jnp.int32)
    raw_key = pair_sum[:, :HEAD_SIZE]
    unrotated = jnp.concatenate([raw_key[:rows]] * perms + [raw_key[rows:]])
    spots = jnp.concatenate([places.reshape(-1), own_tail])
    own_keys = rotate(unrotated[:, None, :], spots)[:, 0, :].astype(jnp.bfloat16)
    own_values = pair_sum[:, HEAD_SIZE:].astype(jnp.bfloat16)
    packed = jnp.concatenate([own_keys, own_values])
    alike = [[k * share + i for i in range(share)] for k in range(kv_heads)]
    every = lax.all_gather(packed, "psg", axis_index_groups=alike)
    cut = perms * rows
    keys = every[:, :cut].reshape(share, perms, rows, HEAD_SIZE)
    tail_keys = every[:, cut : cut + tail_rows].reshape(tail_count, HEAD_SIZE)
    low = cut + tail_rows
    values = every[:, low : low + rows].reshape(total_keys, HEAD_SIZE)
    tail_values = every[:, low + rows :].reshape(tail_count, HEAD_SIZE)

    scale = HEAD_SIZE ** (-0.5)
    scores = (
        jnp.einsum("tgd,spnd->ptgsn", query, keys, preferred_element_type=jnp.float32) * scale
    ).reshape(perms, tail_count, own_heads, total_keys)
    tail_scores = (
        jnp.einsum("tgd,sd->tgs", query, tail_keys, preferred_element_type=jnp.float32) * scale
    )
    causal = jnp.arange(tail_count)[None, :] <= jnp.arange(tail_count)[:, None]
    tail_scores = jnp.where(causal[:, None, :], tail_scores, -1e30)
    peak = jnp.maximum(jnp.max(scores, axis=-1), jnp.max(tail_scores, axis=-1))[..., None]
    weights = jnp.exp(scores - peak)
    tail_weights = jnp.exp(tail_scores - peak)
    denom = jnp.sum(weights, axis=-1) + jnp.sum(tail_weights, axis=-1)
    numer = jnp.einsum(
        "ptgn,nd->ptgd", weights.astype(jnp.bfloat16), values, preferred_element_type=jnp.float32
    ) + jnp.einsum(
        "ptgs,sd->ptgd",
        tail_weights.astype(jnp.bfloat16),
        tail_values,
        preferred_element_type=jnp.float32,
    )
    agreed = jnp.sum(numer / denom[..., None], axis=0)
    own_mixed = agreed.reshape(tail_count, own_heads * HEAD_SIZE).astype(jnp.bfloat16)
    return closing(own_mixed, w_out, norm_gain, shards, width)


def by_rows(
    tail_hidden_states,
    passage_hidden_states,
    lengths,
    storage_order,
    orders,
    w_query,
    key_weight,
    value_weight,
    w_out,
    norm_gain,
):
    shards = lax.axis_size("psg")
    device = lax.axis_index("psg")
    row_count = passage_hidden_states.shape[0]
    tail_count = tail_hidden_states.shape[0]
    kv_heads = key_weight.shape[1] // HEAD_SIZE
    query_heads = w_query.shape[1] // HEAD_SIZE
    query_group = query_heads // kv_heads
    total_keys = row_count * shards
    query_part = jnp.dot(tail_hidden_states, w_query, preferred_element_type=jnp.float32)
    key_part = jnp.dot(tail_hidden_states, key_weight, preferred_element_type=jnp.float32)
    value_part = jnp.dot(tail_hidden_states, value_weight, preferred_element_type=jnp.float32)
    query_sum, key_sum, value_sum = lax.psum((query_part, key_part, value_part), "psg")
    tail_pos = total_keys + jnp.arange(tail_count, dtype=jnp.int32)
    query_vectors = rotate(query_sum.reshape(tail_count, query_heads, HEAD_SIZE), tail_pos).astype(
        jnp.bfloat16
    )
    query_vectors = query_vectors.reshape(tail_count, kv_heads, query_group, HEAD_SIZE)
    tail_key_rows = rotate(key_sum.reshape(tail_count, kv_heads, HEAD_SIZE), tail_pos).astype(
        jnp.bfloat16
    )
    tail_value_rows = value_sum.astype(jnp.bfloat16).reshape(tail_count, kv_heads, HEAD_SIZE)

    def add_block(piece):
        return jnp.dot(passage_hidden_states, piece, preferred_element_type=jnp.float32)

    unrotated_key = add_block(lax.all_gather(key_weight, "psg", axis=0, tiled=True))
    raw_value = add_block(lax.all_gather(value_weight, "psg", axis=0, tiled=True))
    row_ids = device * row_count + jnp.arange(row_count, dtype=jnp.int32)
    token_positions = token_places(lengths, storage_order, orders, row_ids)
    passage_values = raw_value.astype(jnp.bfloat16).reshape(row_count, kv_heads, HEAD_SIZE)
    unrotated_key = unrotated_key.reshape(row_count, kv_heads, HEAD_SIZE)
    scale = HEAD_SIZE ** (-0.5)
    tail_scores = (
        jnp.einsum(
            "tkgd,skd->tkgs", query_vectors, tail_key_rows, preferred_element_type=jnp.float32
        )
        * scale
    )
    causal = jnp.arange(tail_count)[None, :] <= jnp.arange(tail_count)[:, None]
    tail_scores = jnp.where(causal[:, None, None, :], tail_scores, -1e30)
    tail_top = jnp.max(tail_scores, axis=-1)

    def scores_for(places):
        keys = rotate(unrotated_key, places).astype(jnp.bfloat16)
        return (
            jnp.einsum("tkgd,nkd->tkgn", query_vectors, keys, preferred_element_type=jnp.float32)
            * scale
        )

    def local_stats(places):
        scores = scores_for(places)
        peak = jnp.maximum(jnp.max(scores, axis=-1), tail_top)
        return (peak, jnp.sum(jnp.exp(scores - peak[..., None]), axis=-1))

    def combine(first, second):
        peak = jnp.maximum(first[0], second[0])
        return (peak, first[1] * jnp.exp(first[0] - peak) + second[1] * jnp.exp(second[0] - peak))

    peaks, totals = joined(lax.map(local_stats, token_positions), "psg", combine)

    def accumulate(running, inputs):
        places, peak, partial_value = inputs
        weights = jnp.exp(scores_for(places) - peak[..., None])
        tail_weights = jnp.exp(tail_scores - peak[..., None])
        denom = (partial_value + jnp.sum(tail_weights, axis=-1))[..., None]
        shared = jnp.einsum(
            "tkgn,nkd->tkgd",
            weights.astype(jnp.bfloat16),
            passage_values,
            preferred_element_type=jnp.float32,
        )
        own = jnp.einsum(
            "tkgs,skd->tkgd",
            tail_weights.astype(jnp.bfloat16),
            tail_value_rows,
            preferred_element_type=jnp.float32,
        )
        return ((running[0] + shared / denom, running[1] + own / denom), None)

    start_sums = jnp.zeros((tail_count, kv_heads, query_group, HEAD_SIZE), jnp.float32)
    (shared_sum, own_sum), unused_slot = lax.scan(
        accumulate, (start_sums, start_sums), (token_positions, peaks, totals)
    )
    agreed_output = lax.psum(shared_sum, "psg") + own_sum
    mixed = agreed_output.reshape(tail_count, -1).astype(jnp.bfloat16)
    projected = jnp.dot(mixed, w_out, preferred_element_type=jnp.float32)
    squares = lax.psum(jnp.sum(projected * projected, axis=1), "psg")
    factor = lax.rsqrt(squares / MODEL_WIDTH + epsilon)[:, None]
    return (projected * factor * norm_gain[None, :]).astype(jnp.bfloat16)


def per_device(*arrays):
    tail_hidden_states, w_query, key_weight = arrays[0], arrays[5], arrays[6]
    shards = lax.axis_size("psg")
    query_heads = w_query.shape[1] // HEAD_SIZE
    kv_heads = key_weight.shape[1] // HEAD_SIZE
    fits = query_heads % shards == 0 and shards % kv_heads == 0
    fits = fits and shards & (shards - 1) == 0 and tail_hidden_states.shape[0] % 128 == 0
    if fits and tail_hidden_states.shape[0] % (shards // kv_heads) == 0:
        return by_heads(*arrays)
    return by_rows(*arrays)


def solution(mesh):
    placed = (
        P("groups", "psg"),
        P(("groups", "psg"), None),
        P("groups"),
        P("groups"),
        P("groups", None),
        P("psg", None),
        P("psg", None),
        P("psg", None),
        P(None, "psg"),
        P("psg"),
    )
    return jax.shard_map(
        per_device, mesh=mesh, in_specs=placed, out_specs=P("groups", "psg"), check_vma=False
    )
```

```python
import functools

import jax
import jax.numpy as jnp
from jax import lax
from jax.experimental import pallas as pl
from jax.experimental.pallas import tpu as pltpu
from jax.sharding import PartitionSpec as P

MODEL_WIDTH = 8192
HEAD_SIZE = 128


theta_base = 500000.0
epsilon = 1e-05


def joined(part, axis, combine):
    gathered = jax.tree.map(lambda a: lax.all_gather(a, axis), part)

    def take(source):
        return jax.tree.map(lambda a: lax.dynamic_index_in_dim(a, source, 0, False), gathered)

    return lax.fori_loop(
        1, lax.axis_size(axis), lambda source, state: combine(state, take(source)), take(0)
    )


def rotate(vectors, places):
    half = vectors.shape[-1] // 2
    freqs = theta_base ** (-jnp.arange(half, dtype=jnp.float32) * 2.0 / vectors.shape[-1])
    angles = places.astype(jnp.float32)[:, None] * freqs[None, :]
    cosine = jnp.cos(angles)[:, None, :]
    sine = jnp.sin(angles)[:, None, :]
    first = vectors[..., :half]
    second = vectors[..., half:]
    return jnp.concatenate(
        [first * cosine - second * sine, second * cosine + first * sine], axis=-1
    )


def running_sum(values):
    count = values.shape[-1]
    earlier = (jnp.arange(count)[None, :] <= jnp.arange(count)[:, None]).astype(values.dtype)
    return jnp.sum(earlier * values[..., None, :], axis=-1)


def token_places(lengths, storage_order, orders, row_ids):
    numbers = jnp.arange(lengths.shape[0], dtype=jnp.int32)
    pick = (storage_order[:, None] == numbers[None, :]).astype(jnp.int32)
    stored_lengths = jnp.sum(pick * lengths[None, :], axis=1)
    ends = running_sum(stored_lengths)
    starts = ends - stored_lengths
    slots = jnp.sum((ends[None, :] <= row_ids[:, None]).astype(jnp.int32), axis=1)
    in_slot = (slots[:, None] == numbers[None, :]).astype(jnp.int32)
    offsets = row_ids - jnp.sum(in_slot * starts[None, :], axis=1)
    passage_hot = jnp.sum(in_slot[:, :, None] * pick[None, :, :], axis=1)
    ordered_hot = (orders[:, :, None] == numbers[None, None, :]).astype(jnp.int32)
    ordered_lengths = jnp.sum(ordered_hot * lengths[None, None, :], axis=2)
    order_starts = running_sum(ordered_lengths) - ordered_lengths
    placed = jnp.sum(ordered_hot * order_starts[:, :, None], axis=1)
    return jnp.sum(passage_hot[None, :, :] * placed[:, None, :], axis=2) + offsets[None, :]


def backwards(index, bits):
    return sum((index // 2**b) % 2 * 2 ** (bits - 1 - b) for b in range(bits))


def closing_kernel(
    bits, width, own_ref, w_ref, gain_ref, out_ref, held, total, given, got, sends, lands
):
    me = lax.axis_index("psg")
    partners = [me + (1 - 2 * ((me // 2**b) % 2)) * 2**b for b in reversed(range(bits))]
    barrier = pltpu.get_barrier_semaphore()
    for partner in partners:
        pl.semaphore_signal(
            barrier, inc=1, device_id={"psg": partner}, device_id_type=pl.DeviceIdType.MESH
        )
    pl.semaphore_wait(barrier, bits)

    slot = backwards(me, bits)
    held[slot] = own_ref[...]
    for step, partner in enumerate(partners):
        run = pl.ds(slot // 2**step * 2**step, 2**step)
        copy = pltpu.make_async_remote_copy(
            src_ref=held.at[run],
            dst_ref=held.at[run],
            send_sem=sends.at[step],
            recv_sem=lands.at[step],
            device_id={"psg": partner},
            device_id_type=pl.DeviceIdType.MESH,
        )
        copy.start()
        copy.wait()
    part = own_ref.shape[1]
    for j in range(2**bits):
        product = jnp.dot(
            held[backwards(j, bits)],
            w_ref[j * part : (j + 1) * part, :],
            preferred_element_type=jnp.float32,
        )
        if j == 0:
            total[...] = product
        else:
            total[...] += product

    projected = total[...]
    squared = projected * projected
    folded = sum(squared[:, c : c + 128] for c in range(0, squared.shape[1], 128))
    sums = jnp.sum(folded.T, axis=0, keepdims=True)
    for step, partner in enumerate(partners):
        given[step] = jnp.broadcast_to(sums, given.shape[1:])
        copy = pltpu.make_async_remote_copy(
            src_ref=given.at[step],
            dst_ref=got.at[step],
            send_sem=sends.at[bits + step],
            recv_sem=lands.at[bits + step],
            device_id={"psg": partner},
            device_id_type=pl.DeviceIdType.MESH,
        )
        copy.start()
        copy.wait()
        sums = sums + got[step][:1]
    spread = jnp.broadcast_to(sums, (128, sums.shape[1])).T
    factor = lax.rsqrt(spread / width + epsilon)
    for c in range(0, projected.shape[1], 128):
        out_ref[:, c : c + 128] = (
            projected[:, c : c + 128] * factor * gain_ref[:, c : c + 128]
        ).astype(jnp.bfloat16)


def closing(own_mixed, w_out, norm_gain, shards, width):
    bits = shards.bit_length() - 1
    tail_count, columns = own_mixed.shape[0], w_out.shape[1]
    return pl.pallas_call(
        functools.partial(closing_kernel, bits, width),
        out_shape=jax.ShapeDtypeStruct((tail_count, columns), jnp.bfloat16),
        in_specs=[pl.BlockSpec(memory_space=pltpu.VMEM)] * 3,
        out_specs=pl.BlockSpec(memory_space=pltpu.VMEM),
        scratch_shapes=[
            pltpu.VMEM((shards, *own_mixed.shape), jnp.bfloat16),
            pltpu.VMEM((tail_count, columns), jnp.float32),
            pltpu.VMEM((bits, 8, tail_count), jnp.float32),
            pltpu.VMEM((bits, 8, tail_count), jnp.float32),
            pltpu.SemaphoreType.DMA((2 * bits,)),
            pltpu.SemaphoreType.DMA((2 * bits,)),
        ],
        compiler_params=pltpu.CompilerParams(
            collective_id=0, has_side_effects=True, vmem_limit_bytes=32 * 2**20
        ),
    )(own_mixed, w_out, norm_gain[None, :])


def pair_kernel(slab_ref, key_ref, value_ref, out_ref):
    both = jnp.concatenate([key_ref[...], value_ref[...]], axis=1)
    out_ref[0] = jnp.dot(slab_ref[...], both, preferred_element_type=jnp.float32)


def pair_products(slab, key_weight, value_weight):
    count, depth = slab.shape
    kv_heads = key_weight.shape[1] // HEAD_SIZE
    column = pl.BlockSpec((depth, HEAD_SIZE), lambda k: (0, k))
    return pl.pallas_call(
        pair_kernel,
        grid=(kv_heads,),
        out_shape=jax.ShapeDtypeStruct((kv_heads, count, 2 * HEAD_SIZE), jnp.float32),
        in_specs=[pl.BlockSpec((count, depth), lambda k: (0, 0)), column, column],
        out_specs=pl.BlockSpec((1, count, 2 * HEAD_SIZE), lambda k: (k, 0, 0)),
        compiler_params=pltpu.CompilerParams(vmem_limit_bytes=32 * 2**20),
    )(slab, key_weight, value_weight)


def by_heads(
    tail_hidden_states,
    passage_hidden_states,
    lengths,
    storage_order,
    orders,
    w_query,
    key_weight,
    value_weight,
    w_out,
    norm_gain,
):
    shards = lax.axis_size("psg")
    device = lax.axis_index("psg")
    row_count, width = passage_hidden_states.shape
    tail_count, depth = tail_hidden_states.shape
    kv_heads = key_weight.shape[1] // HEAD_SIZE
    own_heads = w_query.shape[1] // HEAD_SIZE // shards
    share = shards // kv_heads
    total_keys = row_count * shards
    rows = total_keys // share
    tail_rows = tail_count // share
    perms = orders.shape[0]
    place = device % share

    query_part = jnp.einsum(
        "td,dsc->stc",
        tail_hidden_states,
        w_query.reshape(depth, shards, own_heads * HEAD_SIZE),
        preferred_element_type=jnp.float32,
    )
    query_part, passage_hidden_states = lax.optimization_barrier(
        (query_part, passage_hidden_states)
    )
    query_sum = lax.psum_scatter(query_part, "psg", scatter_dimension=0)
    slab = lax.all_to_all(passage_hidden_states, "psg", 1, 0, tiled=True)
    slab = jnp.concatenate(
        [slab.reshape(share, rows, depth), tail_hidden_states.reshape(share, tail_rows, depth)],
        axis=1,
    )
    pair_part = pair_products(slab.reshape(-1, depth), key_weight, value_weight)
    query_sum, pair_part = lax.optimization_barrier((query_sum, pair_part))
    pair_sum = lax.psum_scatter(
        pair_part.reshape(shards, rows + tail_rows, 2 * HEAD_SIZE), "psg", scatter_dimension=0
    )

    tail_pos = total_keys + jnp.arange(tail_count, dtype=jnp.int32)
    query = rotate(query_sum.reshape(tail_count, own_heads, HEAD_SIZE), tail_pos)
    query = query.astype(jnp.bfloat16)
    own_rows = place * rows + jnp.arange(rows, dtype=jnp.int32)
    places = token_places(lengths, storage_order, orders, own_rows)
    own_tail = total_keys + place * tail_rows + jnp.arange(tail_rows, dtype=jnp.int32)
    raw_key = pair_sum[:, :HEAD_SIZE]
    unrotated = jnp.concatenate([raw_key[:rows]] * perms + [raw_key[rows:]])
    spots = jnp.concatenate([places.reshape(-1), own_tail])
    own_keys = rotate(unrotated[:, None, :], spots)[:, 0, :].astype(jnp.bfloat16)
    own_values = pair_sum[:, HEAD_SIZE:].astype(jnp.bfloat16)
    packed = jnp.concatenate([own_keys, own_values])
    alike = [[k * share + i for i in range(share)] for k in range(kv_heads)]
    every = lax.all_gather(packed, "psg", axis_index_groups=alike)
    cut = perms * rows
    keys = every[:, :cut].reshape(share, perms, rows, HEAD_SIZE)
    tail_keys = every[:, cut : cut + tail_rows].reshape(tail_count, HEAD_SIZE)
    low = cut + tail_rows
    values = every[:, low : low + rows].reshape(total_keys, HEAD_SIZE)
    tail_values = every[:, low + rows :].reshape(tail_count, HEAD_SIZE)

    scale = HEAD_SIZE ** (-0.5)
    scores = (
        jnp.einsum("tgd,spnd->ptgsn", query, keys, preferred_element_type=jnp.float32) * scale
    ).reshape(perms, tail_count, own_heads, total_keys)
    tail_scores = (
        jnp.einsum("tgd,sd->tgs", query, tail_keys, preferred_element_type=jnp.float32) * scale
    )
    causal = jnp.arange(tail_count)[None, :] <= jnp.arange(tail_count)[:, None]
    tail_scores = jnp.where(causal[:, None, :], tail_scores, -1e30)
    peak = jnp.maximum(jnp.max(scores, axis=-1), jnp.max(tail_scores, axis=-1))[..., None]
    weights = jnp.exp(scores - peak)
    tail_weights = jnp.exp(tail_scores - peak)
    denom = jnp.sum(weights, axis=-1) + jnp.sum(tail_weights, axis=-1)
    numer = jnp.einsum(
        "ptgn,nd->ptgd", weights.astype(jnp.bfloat16), values, preferred_element_type=jnp.float32
    ) + jnp.einsum(
        "ptgs,sd->ptgd",
        tail_weights.astype(jnp.bfloat16),
        tail_values,
        preferred_element_type=jnp.float32,
    )
    agreed = jnp.sum(numer / denom[..., None], axis=0)
    own_mixed = agreed.reshape(tail_count, own_heads * HEAD_SIZE).astype(jnp.bfloat16)
    return closing(own_mixed, w_out, norm_gain, shards, width)


def by_rows(
    tail_hidden_states,
    passage_hidden_states,
    lengths,
    storage_order,
    orders,
    w_query,
    key_weight,
    value_weight,
    w_out,
    norm_gain,
):
    shards = lax.axis_size("psg")
    device = lax.axis_index("psg")
    row_count = passage_hidden_states.shape[0]
    tail_count = tail_hidden_states.shape[0]
    kv_heads = key_weight.shape[1] // HEAD_SIZE
    query_heads = w_query.shape[1] // HEAD_SIZE
    query_group = query_heads // kv_heads
    total_keys = row_count * shards
    query_part = jnp.dot(tail_hidden_states, w_query, preferred_element_type=jnp.float32)
    key_part = jnp.dot(tail_hidden_states, key_weight, preferred_element_type=jnp.float32)
    value_part = jnp.dot(tail_hidden_states, value_weight, preferred_element_type=jnp.float32)
    query_sum, key_sum, value_sum = lax.psum((query_part, key_part, value_part), "psg")
    tail_pos = total_keys + jnp.arange(tail_count, dtype=jnp.int32)
    query_vectors = rotate(query_sum.reshape(tail_count, query_heads, HEAD_SIZE), tail_pos).astype(
        jnp.bfloat16
    )
    query_vectors = query_vectors.reshape(tail_count, kv_heads, query_group, HEAD_SIZE)
    tail_key_rows = rotate(key_sum.reshape(tail_count, kv_heads, HEAD_SIZE), tail_pos).astype(
        jnp.bfloat16
    )
    tail_value_rows = value_sum.astype(jnp.bfloat16).reshape(tail_count, kv_heads, HEAD_SIZE)

    def add_block(piece):
        return jnp.dot(passage_hidden_states, piece, preferred_element_type=jnp.float32)

    unrotated_key = add_block(lax.all_gather(key_weight, "psg", axis=0, tiled=True))
    raw_value = add_block(lax.all_gather(value_weight, "psg", axis=0, tiled=True))
    row_ids = device * row_count + jnp.arange(row_count, dtype=jnp.int32)
    token_positions = token_places(lengths, storage_order, orders, row_ids)
    passage_values = raw_value.astype(jnp.bfloat16).reshape(row_count, kv_heads, HEAD_SIZE)
    unrotated_key = unrotated_key.reshape(row_count, kv_heads, HEAD_SIZE)
    scale = HEAD_SIZE ** (-0.5)
    tail_scores = (
        jnp.einsum(
            "tkgd,skd->tkgs", query_vectors, tail_key_rows, preferred_element_type=jnp.float32
        )
        * scale
    )
    causal = jnp.arange(tail_count)[None, :] <= jnp.arange(tail_count)[:, None]
    tail_scores = jnp.where(causal[:, None, None, :], tail_scores, -1e30)
    tail_top = jnp.max(tail_scores, axis=-1)

    def scores_for(places):
        keys = rotate(unrotated_key, places).astype(jnp.bfloat16)
        return (
            jnp.einsum("tkgd,nkd->tkgn", query_vectors, keys, preferred_element_type=jnp.float32)
            * scale
        )

    def local_stats(places):
        scores = scores_for(places)
        peak = jnp.maximum(jnp.max(scores, axis=-1), tail_top)
        return (peak, jnp.sum(jnp.exp(scores - peak[..., None]), axis=-1))

    def combine(first, second):
        peak = jnp.maximum(first[0], second[0])
        return (peak, first[1] * jnp.exp(first[0] - peak) + second[1] * jnp.exp(second[0] - peak))

    peaks, totals = joined(lax.map(local_stats, token_positions), "psg", combine)

    def accumulate(running, inputs):
        places, peak, partial_value = inputs
        weights = jnp.exp(scores_for(places) - peak[..., None])
        tail_weights = jnp.exp(tail_scores - peak[..., None])
        denom = (partial_value + jnp.sum(tail_weights, axis=-1))[..., None]
        shared = jnp.einsum(
            "tkgn,nkd->tkgd",
            weights.astype(jnp.bfloat16),
            passage_values,
            preferred_element_type=jnp.float32,
        )
        own = jnp.einsum(
            "tkgs,skd->tkgd",
            tail_weights.astype(jnp.bfloat16),
            tail_value_rows,
            preferred_element_type=jnp.float32,
        )
        return ((running[0] + shared / denom, running[1] + own / denom), None)

    start_sums = jnp.zeros((tail_count, kv_heads, query_group, HEAD_SIZE), jnp.float32)
    (shared_sum, own_sum), unused_slot = lax.scan(
        accumulate, (start_sums, start_sums), (token_positions, peaks, totals)
    )
    agreed_output = lax.psum(shared_sum, "psg") + own_sum
    mixed = agreed_output.reshape(tail_count, -1).astype(jnp.bfloat16)
    projected = jnp.dot(mixed, w_out, preferred_element_type=jnp.float32)
    squares = lax.psum(jnp.sum(projected * projected, axis=1), "psg")
    factor = lax.rsqrt(squares / MODEL_WIDTH + epsilon)[:, None]
    return (projected * factor * norm_gain[None, :]).astype(jnp.bfloat16)


def per_device(*arrays):
    tail_hidden_states, w_query, key_weight = arrays[0], arrays[5], arrays[6]
    shards = lax.axis_size("psg")
    query_heads = w_query.shape[1] // HEAD_SIZE
    kv_heads = key_weight.shape[1] // HEAD_SIZE
    fits = query_heads % shards == 0 and shards % kv_heads == 0
    fits = fits and shards & (shards - 1) == 0 and tail_hidden_states.shape[0] % 128 == 0
    if fits and tail_hidden_states.shape[0] % (shards // kv_heads) == 0:
        return by_heads(*arrays)
    return by_rows(*arrays)


def solution(mesh):
    placed = (
        P("groups", "psg"),
        P(("groups", "psg"), None),
        P("groups"),
        P("groups"),
        P("groups", None),
        P("psg", None),
        P("psg", None),
        P("psg", None),
        P(None, "psg"),
        P("psg"),
    )
    return jax.shard_map(
        per_device, mesh=mesh, in_specs=placed, out_specs=P("groups", "psg"), check_vma=False
    )
```
